32 devices in a mesh: lines: 2 (over x), col: 16 (over z, y, core).
Axes of the slice: x: 2, y: 2, z: 4, core: 2. Of those that a mesh axis runs over, the one named last changes fastest.
Arguments:
- primary: float32 [16, 4, 128, 256], P(None, 'lines', 'col'), parts along dimension 1, may hold values from -6 to 6
- conductivity: float32 [128, 512], P('col', 'lines'), parts along dimension 1, may hold values from 0.1 to 10
- wavenumbers: float32 [16], replicated, may hold values from 0.05 to 1.5
- quadrature: float32 [16], replicated, may hold values from 0.02 to 0.2
- electrodes: int32 [64], P(('lines', 'col')), parts along dimension 0, may hold values from 0 to 127, as said below
- far_pole: int32 [4, 32], P('lines'), parts along dimension 0, may hold values from 0 to 31, as said below
- observed: float32 [4, 32], P('lines'), parts along dimension 0, may hold values from -6 to 6
- prior_adjoint: float32 [16, 4, 128, 256], P(None, 'lines', 'col'), parts along dimension 1, may hold values from -0.012 to 0.012
Outputs:
- predicted: float32 [4, 32], P('lines'), parts along dimension 0
- gradient: float32 [128, 512], P('col', 'lines'), parts along dimension 1
The draws below stay inside these ranges and needn't reach their ends.
There are 2 independent parts, one for each index of `lines`. The reference program is written for one: setup_inputs(seed, part) draws one part's arguments, and reference() takes and returns one part's arrays. A program takes and returns all parts, laid end to end along the dimension named above; an argument that names none is the same for every part. Nothing has to cross between parts.
Inputs may be any that keep to these rules, and one draw needn't show every extreme that they name: electrodes[e] lies in columns 4 e to 4 e + 3. far_pole[s, r] differs from r by 1 to 8.
All inputs are finite; a program needn't handle non-finite values.
Results may differ from the reference program's by a relative error of at most 0.0003.
Values sent between devices are 32-bit elements; how exact they have to be, the bound alone decides.
A program may use at most 64 MiB of HBM per device.

```python
import math
import jax
import jax.numpy as jnp
from jax import lax

WAVES = 16
SOURCES = 2
NZ = 256
ITERS = 2
SPREAD = 8
ELECTRODES = 32
NX = 128


def draw_electrodes(key, part):
    numbers = jnp.arange(ELECTRODES)
    shifted = jax.random.randint(key, (ELECTRODES,), 0, 4)
    shifted = jnp.where(numbers == 0, 0, jnp.where(numbers == ELECTRODES - 1, 3, shifted))
    return (4 * numbers + shifted).astype(jnp.int32)


def draw_far_pole(key, part):
    numbers = jnp.arange(ELECTRODES)[None, :]
    spacing = jax.random.randint(jax.random.fold_in(key, 1), (SOURCES, ELECTRODES), 1, SPREAD + 1)
    coin = jax.random.randint(jax.random.fold_in(key, 2), (SOURCES, ELECTRODES), 0, 2)
    forced = (numbers == 1) | (numbers == ELECTRODES - 2)
    spacing = jnp.where(forced, 1, spacing)
    ahead = numbers + spacing
    behind = numbers - spacing
    use_behind = (behind >= 0) & ((coin == 1) | (ahead >= ELECTRODES))
    use_behind = jnp.where(numbers == 1, True, jnp.where(numbers == ELECTRODES - 2, False, use_behind))
    return jnp.where(use_behind, behind, ahead).astype(jnp.int32)


def block_scale(key, shape, shards, least, high):
    factor_of = 1.0
    for dim, parts in shards:
        steps = jax.random.uniform(jax.random.fold_in(jax.random.fold_in(key, 6), dim), (parts,), jnp.float32, least / len(shards), high / len(shards))
        factor_of = factor_of * jnp.repeat(jnp.exp(steps), shape[dim] // parts).reshape((-1,) + (1,) * (len(shape) - 1 - dim))
    return factor_of


def scatter_about(rng, extent, width, most, split=(), kind=jnp.bfloat16):
    gain = block_scale(rng, extent, split, -0.22, 0.18) if split else 1.0
    values = jax.random.normal(rng, extent, jnp.float32) * width * gain
    return jnp.minimum(jnp.maximum(values, -most), most).astype(kind)


def setup_inputs(seed: int = 0, part: int = 0) -> dict:
    keys = jax.random.split(jax.random.key(seed), 9)
    part_keys = jax.random.split(jax.random.fold_in(keys[8], part), 9)
    return {
        "primary": scatter_about(part_keys[0], (WAVES, SOURCES, NX, NZ), 1.0, 6.0, ((2, 16),), jnp.float32),
        "conductivity": jnp.clip(jnp.exp(math.log(10.0) - 4.6051702 * jax.random.uniform(part_keys[1], (NX, NZ), jnp.float32) ** block_scale(part_keys[1], (NX, NZ), ((0, 16),), -0.2, 0.2)), 0.1, 10.0),
        "wavenumbers": jnp.clip(jnp.exp(jax.random.uniform(keys[2], (WAVES,), jnp.float32, math.log(0.05), math.log(1.5))), 0.05, 1.5),
        "quadrature": jnp.clip(jnp.exp(jax.random.uniform(keys[3], (WAVES,), jnp.float32, math.log(0.02), math.log(0.2))), 0.02, 0.2),
        "electrodes": draw_electrodes(jax.random.fold_in(jax.random.fold_in(keys[8], part), 71), part),
        "far_pole": draw_far_pole(jax.random.fold_in(jax.random.fold_in(keys[8], part), 71), part),
        "observed": scatter_about(part_keys[6], (SOURCES, ELECTRODES), 1.0, 6.0, (), jnp.float32),
        "prior_adjoint": scatter_about(part_keys[7], (WAVES, SOURCES, NX, NZ), 0.002, 0.012, ((2, 16),), jnp.float32),
    }


def coefficients(sigma_wide):
    center = sigma_wide[1:-1]
    west_face = 0.5 * (center + sigma_wide[:-2])
    east_face = 0.5 * (center + sigma_wide[2:])
    below_sigma = jnp.concatenate([center[:, 1:], jnp.zeros_like(center[:, :1])], axis=1)
    lower_face = 0.5 * (center + below_sigma)
    above_sigma = jnp.concatenate([jnp.zeros_like(center[:, :1]), center[:, :-1]], axis=1)
    upper_face = 0.5 * (center + above_sigma)
    top_row = jnp.arange(center.shape[1]) == 0
    upper_face = jnp.where(top_row[None, :], 0.0, upper_face)
    return (west_face, east_face, lower_face, upper_face, center)


def stencil(field_wide, faces_set, mass_scale):
    west_face, east_face, lower_face, upper_face, center = faces_set
    middle = field_wide[..., 1:-1, :]
    below_cells = jnp.concatenate([middle[..., 1:], jnp.zeros_like(middle[..., :1])], axis=-1)
    above_cells = jnp.concatenate([jnp.zeros_like(middle[..., :1]), middle[..., :-1]], axis=-1)
    result = west_face * (middle - field_wide[..., :-2, :]) + east_face * (middle - field_wide[..., 2:, :])
    result = result + lower_face * (middle - below_cells) + upper_face * (middle - above_cells)
    return result + mass_scale * center * middle


def conjugate(source, apply_op, start):
    if start is None:
        solution = jnp.zeros_like(source)
        residual = source
    else:
        solution = start
        residual = source - apply_op(start)
    direction = residual
    norm_now = jnp.sum(residual * residual, axis=(1, 2))
    for iteration in range(ITERS):
        applied = apply_op(direction)
        step_size = norm_now / jnp.sum(direction * applied, axis=(1, 2))
        solution = solution + step_size[:, None, None] * direction
        residual = residual - step_size[:, None, None] * applied
        norm_next = jnp.sum(residual * residual, axis=(1, 2))
        direction = residual + (norm_next / norm_now)[:, None, None] * direction
        norm_now = norm_next
    return solution


def reference(primary, conductivity, wavenumbers, quadrature, electrodes, far_pole, observed, prior_adjoint):
    zero_col = jnp.zeros((1, NZ), jnp.float32)
    operator_faces = coefficients(jnp.concatenate([zero_col, conductivity, zero_col], axis=0))
    contrast_faces = coefficients(jnp.concatenate([zero_col, conductivity - 1.0, zero_col], axis=0))

    def pad_field(state):
        edge_zero = jnp.zeros((state.shape[0], 1, NZ), jnp.float32)
        return jnp.concatenate([edge_zero, state, edge_zero], axis=1)

    def forward(primary_k, mass_scale):
        source = -stencil(pad_field(primary_k), contrast_faces, mass_scale)
        secondary = conjugate(source, lambda state: stencil(pad_field(state), operator_faces, mass_scale), None)
        return primary_k + secondary

    def surface_of(inputs_k):
        return forward(inputs_k[0], inputs_k[1] * inputs_k[1])[:, :, 0]

    surfaces = lax.map(surface_of, (primary, wavenumbers))
    weighted = jnp.einsum("k,ksx->sx", quadrature, surfaces, precision=lax.Precision.HIGHEST)
    potentials = jnp.take(weighted, electrodes, axis=1)
    predicted = potentials - jnp.take_along_axis(potentials, far_pole, axis=1)
    misfit = predicted - observed
    source_rows = jnp.arange(SOURCES)[:, None] * jnp.ones_like(far_pole)
    returned = jnp.zeros_like(misfit).at[source_rows, far_pole].add(misfit)
    charge = misfit - returned
    charge_cols = jnp.zeros((SOURCES, NX), jnp.float32).at[:, electrodes].set(charge)
    surface_row = (jnp.arange(NZ) == 0).astype(jnp.float32)

    def accumulate(grad_sum, inputs_k):
        primary_k, wave_k, weight_k, prior_k = inputs_k
        mass_scale = wave_k * wave_k
        total_field = forward(primary_k, mass_scale)
        adjoint_source = weight_k * charge_cols[:, :, None] * surface_row
        adjoint = conjugate(adjoint_source, lambda state: stencil(pad_field(state), operator_faces, mass_scale), prior_k)
        zero_edge = jnp.zeros((SOURCES, 1, NZ), jnp.float32)
        adjoint_next = jnp.concatenate([adjoint[:, 1:], zero_edge], axis=1)
        total_next = jnp.concatenate([total_field[:, 1:], zero_edge], axis=1)
        adjoint_down = jnp.concatenate([adjoint[..., 1:], jnp.zeros_like(adjoint[..., :1])], axis=-1)
        total_down = jnp.concatenate([total_field[..., 1:], jnp.zeros_like(total_field[..., :1])], axis=-1)
        correlation = (adjoint_next - adjoint) * (total_next - total_field)
        correlation = correlation + (adjoint_down - adjoint) * (total_down - total_field)
        correlation = correlation + mass_scale * adjoint * total_field
        return grad_sum + jnp.sum(correlation, axis=0), None

    gradient, unused = lax.scan(accumulate, jnp.zeros((NX, NZ), jnp.float32), (primary, wavenumbers, quadrature, prior_adjoint))
    return (predicted, gradient)
```

```python
import functools

import jax
import jax.numpy as jnp
from jax import lax
from jax.experimental import pallas as pl
from jax.experimental.pallas import tpu as pltpu
from jax.sharding import PartitionSpec as P

HALO = 3
F32 = jnp.float32
MESH = pl.DeviceIdType.MESH


def east_of(v):
    return pltpu.roll(v, v.shape[0] - 1, 0)


def divergence(v, east, lower):
    east_flux = east * (v - east_of(v))
    lower_flux = lower * (v - pltpu.roll(v, v.shape[1] - 1, 1))
    return (east_flux - pltpu.roll(east_flux, 1, 0)) + (lower_flux - pltpu.roll(lower_flux, 1, 1))


def face_set(c):
    lanes = lax.broadcasted_iota(jnp.int32, c.shape, 1)
    bottom = lanes == c.shape[1] - 1
    east = 0.5 * (c + east_of(c))
    lower = jnp.where(bottom, 0.0, 0.5 * (c + pltpu.roll(c, c.shape[1] - 1, 1)))
    return east, lower, jnp.where(bottom, 0.5 * c, 0.0)


def fold(product):
    half = product.shape[1] // 2
    return jnp.sum(product[:, :half] + product[:, half:], axis=0, keepdims=True)


def row_sums(block):
    ones = jnp.ones((8, block.shape[1]), F32)
    return lax.dot_general(
        ones, block, (((1,), (1,)), ((), ())), precision=lax.Precision.HIGHEST, preferred_element_type=F32
    )


def step_weights(m, fields):
    m0 = m
    m1, m2, m3 = (pltpu.roll(m, 128 - j * fields, 1) for j in (1, 2, 3))
    a = m0 / m1
    rr = a * a * m2 - m0
    grown = 1.0 + rr / m0
    curve = grown * grown * m1 - 2.0 * grown * a * m2 + a * a * m3
    later = rr / curve
    return a + later * grown, -later * a


def kernel(
    n, prim_hbm, sig_ref, wav_ref, quad_ref, elec_ref, far_ref, obs_ref, prior_hbm, pred_ref, grad_ref,
    prim, prior, sigw, r0f, w0f, nu, nau, na2u, sums, pay, got, pay2, got2, coef, load_sem, halo_send, halo_recv,
    send1, recv1, send2, recv2,
    pack_pr, pack_pl, pack_ar, pack_al, pack_sr, pack_sl, land_pl, land_pr, land_al, land_ar, land_sl, land_sr,
):
    me = lax.axis_index("col")
    fields, cols, depth = prim_hbm.shape
    waves = wav_ref.shape[0]
    sources = fields // waves
    per = elec_ref.shape[0]
    total_e = n * per

    loads = [
        pltpu.make_async_copy(prim_hbm, prim.at[:, pl.ds(0, cols), :], load_sem.at[0]),
        pltpu.make_async_copy(prior_hbm, prior.at[:, pl.ds(0, cols), :], load_sem.at[1]),
    ]
    for c in loads:
        c.start()

    barrier = pltpu.get_barrier_semaphore()

    def greet(j, carry):
        pl.semaphore_signal(barrier, inc=1, device_id={"col": lax.rem(me + j, n)}, device_id_type=MESH)
        return carry

    lax.fori_loop(1, n, greet, 0)
    sig = sig_ref[...]
    pack_sr[...] = sig[cols - HALO :, :]
    pack_sl[...] = sig[:HALO, :]
    for c in loads:
        c.wait()
    pack_pr[...] = prim[:, cols - HALO : cols, :]
    pack_pl[...] = prim[:, 0:HALO, :]
    pack_ar[...] = prior[:, cols - HALO : cols, :]
    pack_al[...] = prior[:, 0:HALO, :]
    pl.semaphore_wait(barrier, n - 1)

    right, left = lax.rem(me + 1, n), lax.rem(me + n - 1, n)

    def halo_copy(src, dst, index, device):
        return pltpu.make_async_remote_copy(
            src_ref=src, dst_ref=dst, send_sem=halo_send.at[index], recv_sem=halo_recv.at[index],
            device_id={"col": device}, device_id_type=MESH,
        )

    to_right = [
        halo_copy(pack_sr, land_sl, 0, right),
        halo_copy(pack_pr, land_pl, 1, right),
        halo_copy(pack_ar, land_al, 2, right),
    ]
    to_left = [
        halo_copy(pack_sl, land_sr, 3, left),
        halo_copy(pack_pl, land_pr, 4, left),
        halo_copy(pack_al, land_ar, 5, left),
    ]
    has_right, has_left = me < n - 1, me > 0

    for i in range(3):
        @pl.when(has_right)
        def _(i=i):
            to_right[i].start()

        @pl.when(has_left)
        def _(i=i):
            to_left[i].start()

    def arrived(i):
        @pl.when(has_left)
        def _():
            to_right[i].wait_recv()

        @pl.when(has_right)
        def _():
            to_left[i].wait_recv()

    rows = lax.broadcasted_iota(jnp.int32, (8, depth), 0)
    keep_low = (rows < HALO) & has_right
    keep_high = (rows >= 8 - HALO) & has_left
    rows16 = lax.broadcasted_iota(jnp.int32, (16, depth), 0)
    inside_b = (rows16 < 8) | ((rows16 < 8 + HALO) & has_right) | ((rows16 >= 16 - HALO) & has_left)
    inside = jnp.where(inside_b, 1.0, 0.0).astype(F32)
    gap = jnp.zeros((8 - 2 * HALO, depth), F32)

    def outer(low, high):
        tile = jnp.concatenate([low, gap, high], axis=0)
        return jnp.where(keep_low | keep_high, tile, 0.0)

    arrived(0)
    sigw[0:8, :] = sig
    sigw[8:16, :] = outer(land_sr[...], land_sl[...])
    c = sigw[...]
    east, lower, bottom = face_set(c)
    contrast = jnp.where(inside_b, c - 1.0, 0.0)
    c_east, c_lower, c_bottom = face_set(contrast)

    lane8 = lax.broadcasted_iota(jnp.int32, (8, 128), 1)
    row8 = lax.broadcasted_iota(jnp.int32, (8, 128), 0)
    picks = [
        jnp.where((lane8 == 0) & (row8 == elec_ref[e] - me * cols), 1.0, 0.0).astype(F32) for e in range(per)
    ]

    arrived(1)

    def forward(k, carry):
        q = wav_ref[k] * wav_ref[k]
        weight = quad_ref[k]
        diagonal = q * c + bottom
        for s in range(sources):
            ks = k * sources + s
            high = outer(land_pr[ks], land_pl[ks])
            prim[ks, 8:16, :] = high
            v = jnp.concatenate([prim[ks, 0:8, :], high], axis=0)
            r = -(divergence(v, c_east, c_lower) + (q * contrast + c_bottom) * v) * inside
            w = (divergence(r, east, lower) + diagonal * r) * inside
            aw = divergence(w, east, lower) + diagonal * w
            r0f[ks] = r
            w0f[ks] = w
            v8, r8, w8, aw8 = v[:8], r[:8], w[:8], aw[:8]
            for j, product in enumerate((r8 * r8, r8 * w8, w8 * w8, w8 * aw8)):
                sums[0, pl.ds(j * fields + ks, 1), :] = fold(product)
            for e in range(per):
                pick = picks[e] * weight
                for j, field in enumerate((v8, r8, w8)):
                    sums[1 + e, pl.ds(j * fields + ks, 1), :] = jnp.sum(pick * field[:, :128], axis=0, keepdims=True)
        return carry

    lax.fori_loop(0, waves, forward, 0)
    for e in range(per):
        rest = 128 - 3 * fields
        where = jnp.where(
            (lax.broadcasted_iota(jnp.int32, (rest, 128), 0) == 0)
            & (lax.broadcasted_iota(jnp.int32, (rest, 128), 1) == 0),
            elec_ref[e].astype(F32),
            0.0,
        )
        sums[1 + e, 3 * fields :, :] = where
    for g in range(1 + per):
        pay[g : g + 1, :] = row_sums(sums[g])[0:1, :]

    def spread(src, dst, send, recv, j):
        return pltpu.make_async_remote_copy(
            src_ref=src, dst_ref=dst.at[me], send_sem=send.at[j], recv_sem=recv.at[j],
            device_id={"col": lax.rem(me + j, n)}, device_id_type=MESH,
        )

    def collect(src, dst, send, recv, j):
        return pltpu.make_async_remote_copy(
            src_ref=src, dst_ref=dst.at[lax.rem(me + n - j, n)], send_sem=send.at[j], recv_sem=recv.at[j],
            device_id={"col": lax.rem(me + j, n)}, device_id_type=MESH,
        )

    def start_all(src, dst, send, recv):
        def body(j, carry):
            spread(src, dst, send, recv, j).start()
            return carry

        lax.fori_loop(1, n, body, 0)
        dst[me] = src[...]

    def wait_all(src, dst, send, recv):
        def body(j, carry):
            collect(src, dst, send, recv, j).wait_recv()
            return carry

        lax.fori_loop(1, n, body, 0)

    def sent_all(src, dst, send, recv):
        def body(j, carry):
            spread(src, dst, send, recv, j).wait_send()
            return carry

        lax.fori_loop(1, n, body, 0)

    start_all(pay, got, send1, recv1)

    arrived(2)

    def before(k, carry):
        q = wav_ref[k] * wav_ref[k]
        diagonal = q * c + bottom
        for s in range(sources):
            ks = k * sources + s
            high = outer(land_ar[ks], land_al[ks])
            prior[ks, 8:16, :] = high
            v = jnp.concatenate([prior[ks, 0:8, :], high], axis=0)
            r = -(divergence(v, east, lower) + diagonal * v) * inside
            w = (divergence(r, east, lower) + diagonal * r) * inside
            aw = divergence(w, east, lower) + diagonal * w
            nu[ks] = r
            nau[ks] = w
            na2u[ks] = aw[:8, :128]
            half = depth // 2
            r8, w8, aw8 = r[:8, half:], w[:8, half:], aw[:8, half:]
            for j, product in enumerate((r8 * r8, r8 * w8, w8 * w8, w8 * aw8)):
                sums[0, pl.ds(j * fields + ks, 1), :] = jnp.sum(product, axis=0, keepdims=True)
        return carry

    lax.fori_loop(0, waves, before, 0)

    def spread_weights(row, slot):
        at = lax.broadcasted_iota(jnp.int32, (fields, 128), 0) == lax.broadcasted_iota(jnp.int32, (fields, 128), 1)
        column = jnp.sum(jnp.where(at, jnp.broadcast_to(row, (fields, 128)), 0.0), axis=1, keepdims=True)
        coef[slot] = jnp.broadcast_to(column, (fields, depth))

    wait_all(pay, got, send1, recv1)
    m = jnp.sum(got[:, 0, :], axis=0, keepdims=True)
    first, second = step_weights(m, fields)
    lane = lax.broadcasted_iota(jnp.int32, (1, 128), 1)
    scale = jnp.where(
        lane < fields,
        1.0,
        jnp.where(
            lane < 2 * fields,
            pltpu.roll(first, fields, 1),
            jnp.where(lane < 3 * fields, pltpu.roll(second, 2 * fields, 1), 0.0),
        ),
    )
    device_ids = lax.broadcasted_iota(jnp.int32, (n, total_e), 0)
    receivers = lax.broadcasted_iota(jnp.int32, (n, total_e), 1)
    marks = [got[:, 1 + e, :] for e in range(per)]
    lane_n = lax.broadcasted_iota(jnp.int32, (n, 128), 1)
    places = [jnp.sum(jnp.where(lane_n == 3 * fields, marks[e], 0.0), axis=1, keepdims=True) for e in range(per)]
    columns_here = lax.broadcasted_iota(jnp.int32, (n, 128), 1)
    column_of = (me * cols + jnp.where(columns_here < 8 + HALO, columns_here, columns_here - 16)).astype(F32)
    hits = [places[e] == column_of for e in range(per)]
    charges = []
    for s in range(sources):
        scale_s = jnp.where(lax.rem(lane, sources) == s, scale, 0.0)
        pair = []
        row = jnp.zeros((1, total_e), F32)
        for e in range(per):
            potential = jnp.sum(marks[e] * scale_s, axis=1, keepdims=True)
            own_id = device_ids * per + e
            near = jnp.where(receivers == own_id, 1.0, 0.0)
            far = jnp.where(jnp.broadcast_to(far_ref[s : s + 1, :], (n, total_e)) == own_id, 1.0, 0.0)
            pair.append(near - far)
            row = row + jnp.sum(potential * (near - far), axis=0, keepdims=True)
        pred_ref[s : s + 1, :] = row
        misfit = row - obs_ref[s : s + 1, :]
        spots = jnp.zeros((1, 128), F32)
        for e in range(per):
            charge = jnp.sum(pair[e] * misfit, axis=1, keepdims=True)
            spots = spots + jnp.sum(jnp.where(hits[e], charge, 0.0), axis=0, keepdims=True)
        charges.append(spots)

    row16 = lax.broadcasted_iota(jnp.int32, (16, 128), 0)
    lane16 = lax.broadcasted_iota(jnp.int32, (16, 128), 1)
    inside0 = inside[:, :128]
    c0 = c[:, :128]
    east0 = east[:, :128]
    lower0 = jnp.where(lane16 < 127, lower[:, :128], 0.0)
    impulse = []
    for s in range(sources):
        column = jnp.sum(
            jnp.where(lane16 == row16, jnp.broadcast_to(charges[s], (16, 128)), 0.0), axis=1, keepdims=True
        )
        g = jnp.where(lane16 == 0, column, 0.0) * inside0
        b = divergence(g, east0, lower0) * inside0
        d = c0 * g
        impulse.append((g, b, d, divergence(b, east0, lower0), divergence(d, east0, lower0) + c0 * b, c0 * d))

    def after(k, carry):
        q = wav_ref[k] * wav_ref[k]
        weight = quad_ref[k]
        for s in range(sources):
            ks = k * sources + s
            g, b, d, b2, x, d2 = impulse[s]
            r = weight * g + nu[ks, :, 0:128]
            w = weight * (b + q * d) + nau[ks, :, 0:128]
            nu[ks, :, 0:128] = r
            nau[ks, :, 0:128] = w
            aw8 = weight * (b2[:8] + q * (x[:8] + q * d2[:8])) + na2u[ks]
            r8, w8 = r[:8], w[:8]
            for j, product in enumerate((r8 * r8, r8 * w8, w8 * w8, w8 * aw8)):
                at = pl.ds(j * fields + ks, 1)
                sums[0, at, :] = sums[0, at, :] + jnp.sum(product, axis=0, keepdims=True)
        return carry

    lax.fori_loop(0, waves, after, 0)
    pay2[...] = row_sums(sums[0])[0:1, :]
    start_all(pay2, got2, send2, recv2)

    spread_weights(first, 0)
    spread_weights(second, 1)

    def totals(ks, carry):
        prim[ks] = prim[ks] + coef[0, pl.ds(ks, 1), :] * r0f[ks] + coef[1, pl.ds(ks, 1), :] * w0f[ks]
        return carry

    lax.fori_loop(0, fields, totals, 0)
    sent_all(pay, got, send1, recv1)
    for i in range(3):
        @pl.when(has_right)
        def _(i=i):
            to_right[i].wait_send()

        @pl.when(has_left)
        def _(i=i):
            to_left[i].wait_send()

    wait_all(pay2, got2, send2, recv2)
    first, second = step_weights(jnp.sum(got2[:, 0, :], axis=0, keepdims=True), fields)
    spread_weights(first, 0)
    spread_weights(second, 1)
    last = lax.broadcasted_iota(jnp.int32, (8, depth), 1) == depth - 1

    def correlate(k, total):
        q = wav_ref[k] * wav_ref[k]
        for s in range(sources):
            ks = k * sources + s
            t = prim[ks]
            a = prior[ks] + coef[0, pl.ds(ks, 1), :] * nu[ks] + coef[1, pl.ds(ks, 1), :] * nau[ks]
            t_east, a_east = east_of(t)[:8], east_of(a)[:8]
            t, a = t[:8], a[:8]
            t_down = jnp.where(last, 0.0, pltpu.roll(t, depth - 1, 1))
            a_down = jnp.where(last, 0.0, pltpu.roll(a, depth - 1, 1))
            total = total + ((a_east - a) * (t_east - t) + (a_down - a) * (t_down - t) + q * a * t)
        return total

    grad_ref[...] = lax.fori_loop(0, waves, correlate, jnp.zeros((8, depth), F32))
    sent_all(pay2, got2, send2, recv2)


def on_device(n, primary, conductivity, wavenumbers, quadrature, electrodes, far_pole, observed, prior_adjoint):
    waves, sources, cols, depth = primary.shape
    fields = waves * sources
    per = electrodes.shape[0]
    vmem, smem = (pl.BlockSpec(memory_space=m) for m in (pltpu.VMEM, pltpu.SMEM))
    anywhere = pl.BlockSpec(memory_space=pl.ANY)
    wide = pltpu.VMEM((fields, 16, depth), F32)
    edge = pltpu.VMEM((fields, HALO, depth), F32)
    sigma_edge = pltpu.VMEM((HALO, depth), F32)
    dma = pltpu.SemaphoreType.DMA
    return pl.pallas_call(
        functools.partial(kernel, n),
        out_shape=(
            jax.ShapeDtypeStruct(observed.shape, F32),
            jax.ShapeDtypeStruct(conductivity.shape, F32),
        ),
        in_specs=[anywhere, vmem, smem, smem, smem, vmem, vmem, anywhere],
        out_specs=(vmem, vmem),
        scratch_shapes=[
            wide, wide, pltpu.VMEM((16, depth), F32), wide, wide, wide, wide,
            pltpu.VMEM((fields, 8, 128), F32),
            pltpu.VMEM((1 + per, 128, 128), F32),
            pltpu.VMEM((1 + per, 128), F32), pltpu.VMEM((n, 1 + per, 128), F32),
            pltpu.VMEM((1, 128), F32), pltpu.VMEM((n, 1, 128), F32),
            pltpu.VMEM((2, fields, depth), F32),
            dma((2,)), dma((6,)), dma((6,)), dma((n,)), dma((n,)), dma((n,)), dma((n,)),
            edge, edge, edge, edge, sigma_edge, sigma_edge, edge, edge, edge, edge, sigma_edge, sigma_edge,
        ],
        compiler_params=pltpu.CompilerParams(
            collective_id=0, has_side_effects=True, vmem_limit_bytes=32 * 1024 * 1024
        ),
    )(
        primary.reshape(fields, cols, depth), conductivity, wavenumbers, quadrature, electrodes, far_pole, observed,
        prior_adjoint.reshape(fields, cols, depth),
    )


def solution(mesh):
    placed = (
        P(None, "lines", "col", None), P("col", "lines"), P(), P(), P(("lines", "col")),
        P("lines", None), P("lines", None), P(None, "lines", "col", None),
    )
    return jax.shard_map(
        functools.partial(on_device, mesh.shape["col"]),
        mesh=mesh, in_specs=placed, out_specs=(P("lines", None), P("col", "lines")), check_vma=False,
    )
```

```python
import functools

import jax
import jax.numpy as jnp
from jax import lax
from jax.experimental import pallas as pl
from jax.experimental.pallas import tpu as pltpu
from jax.sharding import PartitionSpec as P

LEFT, RIGHT = 2, 3
GROUP = 4
F32 = jnp.float32
MESH = pl.DeviceIdType.MESH


def east_of(v):
    return pltpu.roll(v, v.shape[0] - 1, 0)


def divergence(v, east, lower):
    east_flux = east * (v - east_of(v))
    lower_flux = lower * (v - pltpu.roll(v, v.shape[1] - 1, 1))
    return (east_flux - pltpu.roll(east_flux, 1, 0)) + (lower_flux - pltpu.roll(lower_flux, 1, 1))


def face_set(c):
    lanes = lax.broadcasted_iota(jnp.int32, c.shape, 1)
    bottom = lanes == c.shape[1] - 1
    east = 0.5 * (c + east_of(c))
    lower = jnp.where(bottom, 0.0, 0.5 * (c + pltpu.roll(c, c.shape[1] - 1, 1)))
    return east, lower, jnp.where(bottom, 0.5 * c, 0.0)


def fold(product):
    half = product.shape[1] // 2
    return product[:, :half] + product[:, half:]


def stack_sums(tiles):
    row = lax.broadcasted_iota(jnp.int32, tiles[0].shape, 0)
    low = row < 4
    y = [
        jnp.where(low, tiles[i], tiles[i + 4]) + pltpu.roll(jnp.where(low, tiles[i + 4], tiles[i]), 4, 0)
        for i in range(4)
    ]
    even = (row & 2) == 0
    z = [
        jnp.where(even, y[i] + pltpu.roll(y[i], 6, 0), y[i + 2] + pltpu.roll(y[i + 2], 2, 0)) for i in range(2)
    ]
    return jnp.where((row & 1) == 0, z[0] + pltpu.roll(z[0], 7, 0), z[1] + pltpu.roll(z[1], 1, 0))


def energy(w, east, lower, diagonal):
    across = w - east_of(w)
    down = w - pltpu.roll(w, w.shape[1] - 1, 1)
    return (east * across * across + lower * down * down + diagonal * w * w)[:8]


def row_sums(block):
    ones = jnp.ones((8, block.shape[1]), F32)
    return lax.dot_general(
        ones, block, (((1,), (1,)), ((), ())), precision=lax.Precision.HIGHEST, preferred_element_type=F32
    )


def step_weights(m, sources):
    m0 = m
    m1, m2, m3 = (pltpu.roll(m, 128 - j * sources, 1) for j in (1, 2, 3))
    a = m0 / m1
    rr = a * a * m2 - m0
    grown = 1.0 + rr / m0
    curve = grown * grown * m1 - 2.0 * grown * a * m2 + a * a * m3
    later = rr / curve
    return a + later * grown, -later * a


def kernel(
    n, prim_hbm, sig_hbm, wav_hbm, quad_hbm, elec_hbm, far_hbm, obs_hbm, prior_hbm, pred_ref, grad_ref,
    prim, prior, sigw, wav_ref, quad_ref, elec_ref, far_ref, obs_ref,
    r0f, w0f, nu, nau, sums, pay, got, pay2, got2, coef, load_sem,
    send_r, recv_r, send_l, recv_l, send1, recv1, send2, recv2,
    pack_pr, pack_pl, pack_ar, pack_al, pack_sr, pack_sl, land_pl, land_pr, land_al, land_ar, land_sl, land_sr,
):
    me = lax.axis_index("col")
    fields, cols, depth = prim_hbm.shape
    waves = wav_hbm.shape[0]
    sources = fields // waves
    per = elec_hbm.shape[0]
    total_e = n * per
    chunks = waves // GROUP
    span = GROUP * sources

    loads = [
        pltpu.make_async_copy(src, dst, load_sem.at[i])
        for i, (src, dst) in enumerate((
            (sig_hbm, sigw.at[pl.ds(0, cols), :]),
            (prim_hbm, prim.at[:, pl.ds(0, cols), :]),
            (prior_hbm, prior.at[:, pl.ds(0, cols), :]),
            (wav_hbm, wav_ref), (quad_hbm, quad_ref), (elec_hbm, elec_ref), (far_hbm, far_ref), (obs_hbm, obs_ref),
        ))
    ]
    for copy in loads:
        copy.start()

    barrier = pltpu.get_barrier_semaphore()

    def greet(j, carry):
        pl.semaphore_signal(barrier, inc=1, device_id={"col": lax.rem(me + j, n)}, device_id_type=MESH)
        return carry

    lax.fori_loop(1, n, greet, 0, unroll=n <= 16)
    loads[0].wait()
    sig = sigw[0:8, :]
    pack_sr[...] = sig[cols - LEFT :, :]
    pack_sl[...] = sig[:RIGHT, :]
    loads[1].wait()
    pack_pr[...] = prim[:, cols - LEFT : cols, :]
    pack_pl[...] = prim[:, 0:RIGHT, :]
    pl.semaphore_wait(barrier, n - 1)

    right, left = lax.rem(me + 1, n), lax.rem(me + n - 1, n)
    has_right, has_left = me < n - 1, me > 0

    def both(index, rightward, leftward):
        return (
            pltpu.make_async_remote_copy(
                src_ref=rightward[0], dst_ref=rightward[1], send_sem=send_r.at[index], recv_sem=recv_r.at[index],
                device_id={"col": right}, device_id_type=MESH,
            ),
            pltpu.make_async_remote_copy(
                src_ref=leftward[0], dst_ref=leftward[1], send_sem=send_l.at[index], recv_sem=recv_l.at[index],
                device_id={"col": left}, device_id_type=MESH,
            ),
        )

    def sigma_halo():
        return both(2 * chunks, (pack_sr, land_sl), (pack_sl, land_sr))

    def prim_halo(g):
        at = pl.ds(g * span, span)
        return both(g, (pack_pr.at[at], land_pl.at[at]), (pack_pl.at[at], land_pr.at[at]))

    def prior_halo(g):
        at = pl.ds(g * span, span)
        return both(chunks + g, (pack_ar.at[at], land_al.at[at]), (pack_al.at[at], land_ar.at[at]))

    def start_both(pair):
        @pl.when(has_right)
        def _():
            pair[0].start()

        @pl.when(has_left)
        def _():
            pair[1].start()

    def arrived(pair):
        @pl.when(has_left)
        def _():
            pair[0].wait_recv()

        @pl.when(has_right)
        def _():
            pair[1].wait_recv()

    def sent(pair):
        @pl.when(has_right)
        def _():
            pair[0].wait_send()

        @pl.when(has_left)
        def _():
            pair[1].wait_send()

    start_both(sigma_halo())
    for g in range(chunks):
        start_both(prim_halo(g))
    loads[2].wait()
    pack_ar[...] = prior[:, cols - LEFT : cols, :]
    pack_al[...] = prior[:, 0:RIGHT, :]
    for g in range(chunks):
        start_both(prior_halo(g))
    for copy in loads[3:]:
        copy.wait()

    rows = lax.broadcasted_iota(jnp.int32, (8, depth), 0)
    keep = ((rows < RIGHT) & has_right) | ((rows >= 8 - LEFT) & has_left)
    inside8 = jnp.where(keep, 1.0, 0.0).astype(F32)
    inside = jnp.concatenate([jnp.ones((8, depth), F32), inside8], axis=0)
    gap = jnp.zeros((8 - LEFT - RIGHT, depth), F32)

    def outer(low, high):
        return jnp.where(keep, jnp.concatenate([low, gap, high], axis=0), 0.0)

    def clip(v):
        return jnp.concatenate([v[:8], v[8:] * inside8[:, : v.shape[1]]], axis=0)

    arrived(sigma_halo())
    sigw[8:16, :] = outer(land_sr[...], land_sl[...])
    c = sigw[...]
    east, lower, bottom = face_set(c)
    contrast = (c - 1.0) * inside
    c_east, c_lower, c_bottom = face_set(contrast)
    rows16 = lax.broadcasted_iota(jnp.int32, (16, depth), 0)
    edge = jnp.where((rows16 == 0) & (me == 0), 0.5 * c, 0.0)

    lane8 = lax.broadcasted_iota(jnp.int32, (8, 128), 1)
    row8 = lax.broadcasted_iota(jnp.int32, (8, 128), 0)
    picks = [
        jnp.where((lane8 == 0) & (row8 == elec_ref[e] - me * cols), 1.0, 0.0).astype(F32) for e in range(per)
    ]

    empty = jnp.zeros((8, 128), F32)

    def forward(g, carry):
        arrived(prim_halo(g))
        for step in range(GROUP):
            k = g * GROUP + step
            q = wav_ref[k] * wav_ref[k]
            weight = quad_ref[k]
            diagonal = q * c + bottom
            source_diagonal = q * contrast + c_bottom
            moments, spots = {}, {}
            for s in range(sources):
                ks = k * sources + s
                high = outer(land_pr[ks], land_pl[ks])
                prim[ks, 8:16, :] = high
                v = jnp.concatenate([prim[ks, 0:8, :], high], axis=0)
                r = clip(-(divergence(v, c_east, c_lower) + source_diagonal * v))
                w = clip(divergence(r, east, lower) + diagonal * r)
                r0f[ks] = r
                w0f[ks] = w
                r8, w8 = r[:8], w[:8]
                last_sum = energy(w, east, lower, diagonal + edge)
                for j, product in enumerate((r8 * r8, r8 * w8, w8 * w8, last_sum)):
                    moments[j, s] = fold(product)
                for e in range(per):
                    pick = picks[e] * weight
                    for j, field in enumerate((v, r, w)):
                        spots[e, j, s] = pick * field[:8, :128]
                    spots[e, 3, s] = empty
            at = pl.ds(pl.multiple_of(k * 8, 8), 8)
            order = [(j, s) for j in range(4) for s in range(sources)]
            sums[0, at, :] = stack_sums([moments[o] for o in order])
            for e in range(per):
                sums[1 + e, at, :] = stack_sums([spots[(e, *o)] for o in order])
        return carry

    lax.fori_loop(0, chunks, forward, 0)
    mark = 3 * sources
    for e in range(per):
        first_cell = (row8 == mark) & (lane8 == 0)
        sums[1 + e, 0:8, :] = sums[1 + e, 0:8, :] + jnp.where(first_cell, elec_ref[e].astype(F32), 0.0)
    for g in range(1 + per):
        pay[g : g + 1, :] = row_sums(sums[g])[0:1, :]

    def spread(src, dst, send, recv, j):
        return pltpu.make_async_remote_copy(
            src_ref=src, dst_ref=dst.at[me], send_sem=send.at[j], recv_sem=recv.at[j],
            device_id={"col": lax.rem(me + j, n)}, device_id_type=MESH,
        )

    def collect(src, dst, send, recv, j):
        return pltpu.make_async_remote_copy(
            src_ref=src, dst_ref=dst.at[lax.rem(me + n - j, n)], send_sem=send.at[j], recv_sem=recv.at[j],
            device_id={"col": lax.rem(me + j, n)}, device_id_type=MESH,
        )

    def start_all(src, dst, send, recv):
        def body(j, carry):
            spread(src, dst, send, recv, j).start()
            return carry

        lax.fori_loop(1, n, body, 0, unroll=n <= 16)
        dst[me] = src[...]

    def wait_all(src, dst, send, recv):
        def body(j, carry):
            collect(src, dst, send, recv, j).wait_recv()
            return carry

        lax.fori_loop(1, n, body, 0, unroll=n <= 16)

    def sent_all(src, dst, send, recv):
        def body(j, carry):
            spread(src, dst, send, recv, j).wait_send()
            return carry

        lax.fori_loop(1, n, body, 0, unroll=n <= 16)

    start_all(pay, got, send1, recv1)

    half = depth // 2

    def before(g, carry):
        arrived(prior_halo(g))
        for step in range(GROUP):
            k = g * GROUP + step
            q = wav_ref[k] * wav_ref[k]
            diagonal = q * c + bottom
            moments = {}
            for s in range(sources):
                ks = k * sources + s
                high = outer(land_ar[ks], land_al[ks])
                prior[ks, 8:16, :] = high
                v = jnp.concatenate([prior[ks, 0:8, :], high], axis=0)
                r = clip(-(divergence(v, east, lower) + diagonal * v))
                w = clip(divergence(r, east, lower) + diagonal * r)
                nu[ks] = r
                nau[ks] = w
                r8, w8 = r[:8, half:], w[:8, half:]
                last_sum = energy(w, east, lower, diagonal + edge)[:, half:]
                for j, product in enumerate((r8 * r8, r8 * w8, w8 * w8, last_sum)):
                    moments[j, s] = product
            at = pl.ds(pl.multiple_of(k * 8, 8), 8)
            sums[0, at, :] = stack_sums([moments[j, s] for j in range(4) for s in range(sources)])
        return carry

    lax.fori_loop(0, chunks, before, 0)

    def spread_weights(row, slot):
        ks = lax.broadcasted_iota(jnp.int32, (fields, 128), 0)
        lanes = lax.broadcasted_iota(jnp.int32, (fields, 128), 1)
        at = lanes == lax.div(ks, sources) * 8 + lax.rem(ks, sources)
        column = jnp.sum(jnp.where(at, jnp.broadcast_to(row, (fields, 128)), 0.0), axis=1, keepdims=True)
        coef[slot] = jnp.broadcast_to(column, (fields, depth))

    wait_all(pay, got, send1, recv1)
    m = jnp.sum(got[:, 0, :], axis=0, keepdims=True)
    first, second = step_weights(m, sources)
    lane = lax.broadcasted_iota(jnp.int32, (1, 128), 1)
    part = lax.div(lax.rem(lane, 8), sources)
    scale = jnp.where(
        part == 0,
        1.0,
        jnp.where(
            part == 1,
            pltpu.roll(first, sources, 1),
            jnp.where(part == 2, pltpu.roll(second, 2 * sources, 1), 0.0),
        ),
    )
    device_ids = lax.broadcasted_iota(jnp.int32, (n, total_e), 0)
    receivers = lax.broadcasted_iota(jnp.int32, (n, total_e), 1)
    marks = [got[:, 1 + e, :] for e in range(per)]
    lane_n = lax.broadcasted_iota(jnp.int32, (n, 128), 1)
    places = [jnp.sum(jnp.where(lane_n == mark, marks[e], 0.0), axis=1, keepdims=True) for e in range(per)]
    columns_here = lax.broadcasted_iota(jnp.int32, (n, 128), 1)
    column_of = (me * cols + jnp.where(columns_here < 8 + RIGHT, columns_here, columns_here - 16)).astype(F32)
    hits = [places[e] == column_of for e in range(per)]
    charges = []
    for s in range(sources):
        scale_s = jnp.where(lax.rem(lane, sources) == s, scale, 0.0)
        pair = []
        row = jnp.zeros((1, total_e), F32)
        for e in range(per):
            potential = jnp.sum(marks[e] * scale_s, axis=1, keepdims=True)
            own_id = device_ids * per + e
            near = jnp.where(receivers == own_id, 1.0, 0.0)
            far = jnp.where(jnp.broadcast_to(far_ref[s : s + 1, :], (n, total_e)) == own_id, 1.0, 0.0)
            pair.append(near - far)
            row = row + jnp.sum(potential * (near - far), axis=0, keepdims=True)
        pred_ref[s : s + 1, :] = row
        misfit = row - obs_ref[s : s + 1, :]
        spots = jnp.zeros((1, 128), F32)
        for e in range(per):
            charge = jnp.sum(pair[e] * misfit, axis=1, keepdims=True)
            spots = spots + jnp.sum(jnp.where(hits[e], charge, 0.0), axis=0, keepdims=True)
        charges.append(spots)

    row16 = lax.broadcasted_iota(jnp.int32, (16, 128), 0)
    lane16 = lax.broadcasted_iota(jnp.int32, (16, 128), 1)
    inside0 = inside[:, :128]
    c0 = c[:, :128]
    east0 = east[:, :128]
    lower0 = jnp.where(lane16 < 127, lower[:, :128], 0.0)
    impulse = []
    for s in range(sources):
        column = jnp.sum(
            jnp.where(lane16 == row16, jnp.broadcast_to(charges[s], (16, 128)), 0.0), axis=1, keepdims=True
        )
        g = jnp.where(lane16 == 0, column, 0.0) * inside0
        b = divergence(g, east0, lower0) * inside0
        d = c0 * g
        impulse.append((g, b, c0 * g))

    def after(g, carry):
        for step in range(GROUP):
            k = g * GROUP + step
            q = wav_ref[k] * wav_ref[k]
            weight = quad_ref[k]
            diagonal = q * c + bottom + edge
            moments = {}
            for s in range(sources):
                ks = k * sources + s
                point, b, d = impulse[s]
                r = weight * point + nu[ks, :, 0:128]
                w = weight * (b + q * d) + nau[ks, :, 0:128]
                nu[ks, :, 0:128] = r
                nau[ks, :, 0:128] = w
                r8, w8 = r[:8], w[:8]
                whole = jnp.concatenate([w, nau[ks, :, half:]], axis=1)
                last_sum = energy(whole, east, lower, diagonal)[:, :128]
                for j, product in enumerate((r8 * r8, r8 * w8, w8 * w8, last_sum)):
                    moments[j, s] = product
            at = pl.ds(pl.multiple_of(k * 8, 8), 8)
            sums[0, at, :] = sums[0, at, :] + stack_sums([moments[j, s] for j in range(4) for s in range(sources)])
        return carry

    lax.fori_loop(0, chunks, after, 0)
    pay2[...] = row_sums(sums[0])[0:1, :]
    start_all(pay2, got2, send2, recv2)

    spread_weights(first, 0)
    spread_weights(second, 1)

    def totals(g, carry):
        for step in range(span):
            ks = g * span + step
            prim[ks] = prim[ks] + coef[0, pl.ds(ks, 1), :] * r0f[ks] + coef[1, pl.ds(ks, 1), :] * w0f[ks]
        return carry

    lax.fori_loop(0, chunks, totals, 0)
    sent_all(pay, got, send1, recv1)
    sent(sigma_halo())
    for g in range(chunks):
        sent(prim_halo(g))
        sent(prior_halo(g))

    wait_all(pay2, got2, send2, recv2)
    first, second = step_weights(jnp.sum(got2[:, 0, :], axis=0, keepdims=True), sources)
    spread_weights(first, 0)
    spread_weights(second, 1)
    last = lax.broadcasted_iota(jnp.int32, (8, depth), 1) == depth - 1

    def correlate(g, total):
        for step in range(GROUP):
            k = g * GROUP + step
            q = wav_ref[k] * wav_ref[k]
            for s in range(sources):
                ks = k * sources + s
                t = prim[ks]
                a = prior[ks] + coef[0, pl.ds(ks, 1), :] * nu[ks] + coef[1, pl.ds(ks, 1), :] * nau[ks]
                t_east, a_east = east_of(t)[:8], east_of(a)[:8]
                t, a = t[:8], a[:8]
                t_down = jnp.where(last, 0.0, pltpu.roll(t, depth - 1, 1))
                a_down = jnp.where(last, 0.0, pltpu.roll(a, depth - 1, 1))
                total = total + ((a_east - a) * (t_east - t) + (a_down - a) * (t_down - t) + q * a * t)
        return total

    grad_ref[...] = lax.fori_loop(0, chunks, correlate, jnp.zeros((8, depth), F32))
    sent_all(pay2, got2, send2, recv2)


def on_device(n, primary, conductivity, wavenumbers, quadrature, electrodes, far_pole, observed, prior_adjoint):
    waves, sources, cols, depth = primary.shape
    fields = waves * sources
    per = electrodes.shape[0]
    vmem = pl.BlockSpec(memory_space=pltpu.VMEM)
    anywhere = pl.BlockSpec(memory_space=pl.ANY)
    wide = pltpu.VMEM((fields, 16, depth), F32)

    def edges(count):
        return pltpu.VMEM((fields, count, depth), F32)

    def sigma_edges(count):
        return pltpu.VMEM((count, depth), F32)

    dma = pltpu.SemaphoreType.DMA
    halos = 2 * (waves // GROUP) + 1
    return pl.pallas_call(
        functools.partial(kernel, n),
        out_shape=(
            jax.ShapeDtypeStruct(observed.shape, F32),
            jax.ShapeDtypeStruct(conductivity.shape, F32),
        ),
        in_specs=[anywhere] * 8,
        out_specs=(vmem, vmem),
        scratch_shapes=[
            wide, wide, pltpu.VMEM((16, depth), F32),
            pltpu.SMEM((waves,), F32), pltpu.SMEM((waves,), F32), pltpu.SMEM((per,), jnp.int32),
            pltpu.VMEM(far_pole.shape, jnp.int32), pltpu.VMEM(observed.shape, F32),
            wide, wide, wide, wide,
            pltpu.VMEM((1 + per, 128, 128), F32),
            pltpu.VMEM((1 + per, 128), F32), pltpu.VMEM((n, 1 + per, 128), F32),
            pltpu.VMEM((1, 128), F32), pltpu.VMEM((n, 1, 128), F32),
            pltpu.VMEM((2, fields, depth), F32),
            dma((8,)), dma((halos,)), dma((halos,)), dma((halos,)), dma((halos,)), dma((n,)), dma((n,)), dma((n,)), dma((n,)),
            edges(LEFT), edges(RIGHT), edges(LEFT), edges(RIGHT), sigma_edges(LEFT), sigma_edges(RIGHT),
            edges(LEFT), edges(RIGHT), edges(LEFT), edges(RIGHT), sigma_edges(LEFT), sigma_edges(RIGHT),
        ],
        compiler_params=pltpu.CompilerParams(
            collective_id=0, has_side_effects=True, vmem_limit_bytes=56 * 1024 * 1024
        ),
    )(
        primary.reshape(fields, cols, depth), conductivity, wavenumbers, quadrature, electrodes, far_pole, observed,
        prior_adjoint.reshape(fields, cols, depth),
    )


def solution(mesh):
    placed = (
        P(None, "lines", "col", None), P("col", "lines"), P(), P(), P(("lines", "col")),
        P("lines", None), P("lines", None), P(None, "lines", "col", None),
    )
    return jax.shard_map(
        functools.partial(on_device, mesh.shape["col"]),
        mesh=mesh, in_specs=placed, out_specs=(P("lines", None), P("col", "lines")), check_vma=False,
    )
```

```python
import functools

import jax
import jax.numpy as jnp
from jax import lax
from jax.experimental import pallas as pl
from jax.experimental.pallas import tpu as pltpu
from jax.sharding import PartitionSpec as P

LEFT, RIGHT = 2, 3
GROUP = 4
F32 = jnp.float32
MESH = pl.DeviceIdType.MESH


def east_of(v):
    return pltpu.roll(v, v.shape[0] - 1, 0)


def divergence(v, east, lower):
    east_flux = east * (v - east_of(v))
    lower_flux = lower * (v - pltpu.roll(v, v.shape[1] - 1, 1))
    return (east_flux - pltpu.roll(east_flux, 1, 0)) + (lower_flux - pltpu.roll(lower_flux, 1, 1))


def face_set(c):
    lanes = lax.broadcasted_iota(jnp.int32, c.shape, 1)
    bottom = lanes == c.shape[1] - 1
    east = 0.5 * (c + east_of(c))
    lower = jnp.where(bottom, 0.0, 0.5 * (c + pltpu.roll(c, c.shape[1] - 1, 1)))
    return east, lower, jnp.where(bottom, 0.5 * c, 0.0)


def fold(product):
    half = product.shape[1] // 2
    return product[:, :half] + product[:, half:]


def stack_sums(tiles):
    row = lax.broadcasted_iota(jnp.int32, tiles[0].shape, 0)
    low = row < 4
    y = [
        jnp.where(low, tiles[i], tiles[i + 4]) + pltpu.roll(jnp.where(low, tiles[i + 4], tiles[i]), 4, 0)
        for i in range(4)
    ]
    even = (row & 2) == 0
    z = [
        jnp.where(even, y[i] + pltpu.roll(y[i], 6, 0), y[i + 2] + pltpu.roll(y[i + 2], 2, 0)) for i in range(2)
    ]
    return jnp.where((row & 1) == 0, z[0] + pltpu.roll(z[0], 7, 0), z[1] + pltpu.roll(z[1], 1, 0))


def energy(w, east, lower, diagonal):
    across = w - east_of(w)
    down = w - pltpu.roll(w, w.shape[1] - 1, 1)
    return (east * across * across + lower * down * down + diagonal * w * w)[:8]


def row_sums(block):
    ones = jnp.ones((8, block.shape[1]), F32)
    return lax.dot_general(
        ones, block, (((1,), (1,)), ((), ())), precision=lax.Precision.HIGHEST, preferred_element_type=F32
    )


def step_weights(m, sources):
    m0 = m
    m1, m2, m3 = (pltpu.roll(m, 128 - j * sources, 1) for j in (1, 2, 3))
    a = m0 / m1
    rr = a * a * m2 - m0
    grown = 1.0 + rr / m0
    curve = grown * grown * m1 - 2.0 * grown * a * m2 + a * a * m3
    later = rr / curve
    return a + later * grown, -later * a


def kernel(
    n, prim_hbm, sig_hbm, wav_hbm, quad_hbm, elec_hbm, far_hbm, obs_hbm, prior_hbm, pred_ref, grad_ref,
    prim, prior, sigw, wav_ref, quad_ref, elec_ref, far_ref, obs_ref,
    r0f, w0f, nu, nau, sums, pay, got, pay2, got2, coef, load_sem,
    send_r, recv_r, send_l, recv_l, send1, recv1, send2, recv2,
    pack_pr, pack_pl, pack_ar, pack_al, pack_sr, pack_sl, land_pl, land_pr, land_al, land_ar, land_sl, land_sr,
):
    me = lax.axis_index("col")
    fields, cols, depth = prim_hbm.shape
    waves = wav_hbm.shape[0]
    sources = fields // waves
    per = elec_hbm.shape[0]
    total_e = n * per
    chunks = waves // GROUP
    span = GROUP * sources

    loads = [
        pltpu.make_async_copy(src, dst, load_sem.at[i])
        for i, (src, dst) in enumerate((
            (sig_hbm, sigw.at[pl.ds(0, cols), :]),
            (prim_hbm, prim.at[:, pl.ds(0, cols), :]),
            (prior_hbm, prior.at[:, pl.ds(0, cols), :]),
            (wav_hbm, wav_ref), (quad_hbm, quad_ref), (elec_hbm, elec_ref), (far_hbm, far_ref), (obs_hbm, obs_ref),
        ))
    ]
    for copy in loads:
        copy.start()

    barrier = pltpu.get_barrier_semaphore()

    def greet(j, carry):
        pl.semaphore_signal(barrier, inc=1, device_id={"col": lax.rem(me + j, n)}, device_id_type=MESH)
        return carry

    lax.fori_loop(1, n, greet, 0, unroll=n <= 16)
    loads[0].wait()
    sig = sigw[0:8, :]
    pack_sr[...] = sig[cols - LEFT :, :]
    pack_sl[...] = sig[:RIGHT, :]
    loads[1].wait()
    pack_pr[...] = prim[:, cols - LEFT : cols, :]
    pack_pl[...] = prim[:, 0:RIGHT, :]
    pl.semaphore_wait(barrier, n - 1)

    right, left = lax.rem(me + 1, n), lax.rem(me + n - 1, n)
    has_right, has_left = me < n - 1, me > 0

    def both(index, rightward, leftward):
        return (
            pltpu.make_async_remote_copy(
                src_ref=rightward[0], dst_ref=rightward[1], send_sem=send_r.at[index], recv_sem=recv_r.at[index],
                device_id={"col": right}, device_id_type=MESH,
            ),
            pltpu.make_async_remote_copy(
                src_ref=leftward[0], dst_ref=leftward[1], send_sem=send_l.at[index], recv_sem=recv_l.at[index],
                device_id={"col": left}, device_id_type=MESH,
            ),
        )

    def sigma_halo():
        return both(2 * chunks, (pack_sr, land_sl), (pack_sl, land_sr))

    def prim_halo(g):
        at = pl.ds(g * span, span)
        return both(g, (pack_pr.at[at], land_pl.at[at]), (pack_pl.at[at], land_pr.at[at]))

    def prior_halo(g):
        at = pl.ds(g * span, span)
        return both(chunks + g, (pack_ar.at[at], land_al.at[at]), (pack_al.at[at], land_ar.at[at]))

    def start_both(pair):
        @pl.when(has_right)
        def _():
            pair[0].start()

        @pl.when(has_left)
        def _():
            pair[1].start()

    def arrived(pair):
        @pl.when(has_left)
        def _():
            pair[0].wait_recv()

        @pl.when(has_right)
        def _():
            pair[1].wait_recv()

    def sent(pair):
        @pl.when(has_right)
        def _():
            pair[0].wait_send()

        @pl.when(has_left)
        def _():
            pair[1].wait_send()

    start_both(sigma_halo())
    for g in range(chunks):
        start_both(prim_halo(g))
    loads[2].wait()
    pack_ar[...] = prior[:, cols - LEFT : cols, :]
    pack_al[...] = prior[:, 0:RIGHT, :]
    for copy in loads[3:]:
        copy.wait()

    rows = lax.broadcasted_iota(jnp.int32, (8, depth), 0)
    keep = ((rows < RIGHT) & has_right) | ((rows >= 8 - LEFT) & has_left)
    inside8 = jnp.where(keep, 1.0, 0.0).astype(F32)
    inside = jnp.concatenate([jnp.ones((8, depth), F32), inside8], axis=0)
    gap = jnp.zeros((8 - LEFT - RIGHT, depth), F32)

    def outer(low, high):
        return jnp.where(keep, jnp.concatenate([low, gap, high], axis=0), 0.0)

    def clip(v):
        return jnp.concatenate([v[:8], v[8:] * inside8[:, : v.shape[1]]], axis=0)

    arrived(sigma_halo())
    sigw[8:16, :] = outer(land_sr[...], land_sl[...])
    c = sigw[...]
    east, lower, bottom = face_set(c)
    contrast = (c - 1.0) * inside
    c_east, c_lower, c_bottom = face_set(contrast)
    rows16 = lax.broadcasted_iota(jnp.int32, (16, depth), 0)
    edge = jnp.where((rows16 == 0) & (me == 0), 0.5 * c, 0.0)

    lane8 = lax.broadcasted_iota(jnp.int32, (8, 128), 1)
    row8 = lax.broadcasted_iota(jnp.int32, (8, 128), 0)
    picks = [
        jnp.where((lane8 == 0) & (row8 == elec_ref[e] - me * cols), 1.0, 0.0).astype(F32) for e in range(per)
    ]

    empty = jnp.zeros((8, 128), F32)

    def forward(g, carry):
        arrived(prim_halo(g))
        for step in range(GROUP):
            k = g * GROUP + step
            q = wav_ref[k] * wav_ref[k]
            weight = quad_ref[k]
            diagonal = q * c + bottom
            source_diagonal = q * contrast + c_bottom
            moments, spots = {}, {}
            for s in range(sources):
                ks = k * sources + s
                high = outer(land_pr[ks], land_pl[ks])
                prim[ks, 8:16, :] = high
                v = jnp.concatenate([prim[ks, 0:8, :], high], axis=0)
                r = clip(-(divergence(v, c_east, c_lower) + source_diagonal * v))
                w = clip(divergence(r, east, lower) + diagonal * r)
                r0f[ks] = r
                w0f[ks] = w
                r8, w8 = r[:8], w[:8]
                last_sum = energy(w, east, lower, diagonal + edge)
                for j, product in enumerate((r8 * r8, r8 * w8, w8 * w8, last_sum)):
                    moments[j, s] = fold(product)
                for e in range(per):
                    pick = picks[e] * weight
                    for j, field in enumerate((v, r, w)):
                        spots[e, j, s] = pick * field[:8, :128]
                    spots[e, 3, s] = empty
            at = pl.ds(pl.multiple_of(k * 8, 8), 8)
            order = [(j, s) for j in range(4) for s in range(sources)]
            sums[0, at, :] = stack_sums([moments[o] for o in order])
            for e in range(per):
                sums[1 + e, at, :] = stack_sums([spots[(e, *o)] for o in order])
        return carry

    lax.fori_loop(0, chunks, forward, 0)
    mark = 3 * sources
    for e in range(per):
        first_cell = (row8 == mark) & (lane8 == 0)
        sums[1 + e, 0:8, :] = sums[1 + e, 0:8, :] + jnp.where(first_cell, elec_ref[e].astype(F32), 0.0)
    for g in range(1 + per):
        pay[g : g + 1, :] = row_sums(sums[g])[0:1, :]

    def spread(src, dst, send, recv, j):
        return pltpu.make_async_remote_copy(
            src_ref=src, dst_ref=dst.at[me], send_sem=send.at[j], recv_sem=recv.at[j],
            device_id={"col": lax.rem(me + j, n)}, device_id_type=MESH,
        )

    def collect(src, dst, send, recv, j):
        return pltpu.make_async_remote_copy(
            src_ref=src, dst_ref=dst.at[lax.rem(me + n - j, n)], send_sem=send.at[j], recv_sem=recv.at[j],
            device_id={"col": lax.rem(me + j, n)}, device_id_type=MESH,
        )

    def start_all(src, dst, send, recv):
        def body(j, carry):
            spread(src, dst, send, recv, j).start()
            return carry

        lax.fori_loop(1, n, body, 0, unroll=n <= 16)
        dst[me] = src[...]

    def wait_all(src, dst, send, recv):
        def body(j, carry):
            collect(src, dst, send, recv, j).wait_recv()
            return carry

        lax.fori_loop(1, n, body, 0, unroll=n <= 16)

    def sent_all(src, dst, send, recv):
        def body(j, carry):
            spread(src, dst, send, recv, j).wait_send()
            return carry

        lax.fori_loop(1, n, body, 0, unroll=n <= 16)

    start_all(pay, got, send1, recv1)
    for g in range(chunks):
        start_both(prior_halo(g))

    half = depth // 2

    def before(g, carry):
        arrived(prior_halo(g))
        for step in range(GROUP):
            k = g * GROUP + step
            q = wav_ref[k] * wav_ref[k]
            diagonal = q * c + bottom
            moments = {}
            for s in range(sources):
                ks = k * sources + s
                high = outer(land_ar[ks], land_al[ks])
                prior[ks, 8:16, :] = high
                v = jnp.concatenate([prior[ks, 0:8, :], high], axis=0)
                r = clip(-(divergence(v, east, lower) + diagonal * v))
                w = clip(divergence(r, east, lower) + diagonal * r)
                nu[ks] = r
                nau[ks] = w
                r8, w8 = r[:8, half:], w[:8, half:]
                last_sum = energy(w, east, lower, diagonal + edge)[:, half:]
                for j, product in enumerate((r8 * r8, r8 * w8, w8 * w8, last_sum)):
                    moments[j, s] = product
            at = pl.ds(pl.multiple_of(k * 8, 8), 8)
            sums[0, at, :] = stack_sums([moments[j, s] for j in range(4) for s in range(sources)])
        return carry

    lax.fori_loop(0, chunks, before, 0)

    def spread_weights(row, slot):
        ks = lax.broadcasted_iota(jnp.int32, (fields, 128), 0)
        lanes = lax.broadcasted_iota(jnp.int32, (fields, 128), 1)
        at = lanes == lax.div(ks, sources) * 8 + lax.rem(ks, sources)
        column = jnp.sum(jnp.where(at, jnp.broadcast_to(row, (fields, 128)), 0.0), axis=1, keepdims=True)
        coef[slot] = jnp.broadcast_to(column, (fields, depth))

    wait_all(pay, got, send1, recv1)
    m = jnp.sum(got[:, 0, :], axis=0, keepdims=True)
    first, second = step_weights(m, sources)
    lane = lax.broadcasted_iota(jnp.int32, (1, 128), 1)
    part = lax.div(lax.rem(lane, 8), sources)
    scale = jnp.where(
        part == 0,
        1.0,
        jnp.where(
            part == 1,
            pltpu.roll(first, sources, 1),
            jnp.where(part == 2, pltpu.roll(second, 2 * sources, 1), 0.0),
        ),
    )
    device_ids = lax.broadcasted_iota(jnp.int32, (n, total_e), 0)
    receivers = lax.broadcasted_iota(jnp.int32, (n, total_e), 1)
    marks = [got[:, 1 + e, :] for e in range(per)]
    lane_n = lax.broadcasted_iota(jnp.int32, (n, 128), 1)
    places = [jnp.sum(jnp.where(lane_n == mark, marks[e], 0.0), axis=1, keepdims=True) for e in range(per)]
    columns_here = lax.broadcasted_iota(jnp.int32, (n, 128), 1)
    column_of = (me * cols + jnp.where(columns_here < 8 + RIGHT, columns_here, columns_here - 16)).astype(F32)
    hits = [places[e] == column_of for e in range(per)]
    charges = []
    for s in range(sources):
        scale_s = jnp.where(lax.rem(lane, sources) == s, scale, 0.0)
        pair = []
        row = jnp.zeros((1, total_e), F32)
        for e in range(per):
            potential = jnp.sum(marks[e] * scale_s, axis=1, keepdims=True)
            own_id = device_ids * per + e
            near = jnp.where(receivers == own_id, 1.0, 0.0)
            far = jnp.where(jnp.broadcast_to(far_ref[s : s + 1, :], (n, total_e)) == own_id, 1.0, 0.0)
            pair.append(near - far)
            row = row + jnp.sum(potential * (near - far), axis=0, keepdims=True)
        pred_ref[s : s + 1, :] = row
        misfit = row - obs_ref[s : s + 1, :]
        spots = jnp.zeros((1, 128), F32)
        for e in range(per):
            charge = jnp.sum(pair[e] * misfit, axis=1, keepdims=True)
            spots = spots + jnp.sum(jnp.where(hits[e], charge, 0.0), axis=0, keepdims=True)
        charges.append(spots)

    row16 = lax.broadcasted_iota(jnp.int32, (16, 128), 0)
    lane16 = lax.broadcasted_iota(jnp.int32, (16, 128), 1)
    inside0 = inside[:, :128]
    c0 = c[:, :128]
    east0 = east[:, :128]
    lower0 = jnp.where(lane16 < 127, lower[:, :128], 0.0)
    impulse = []
    for s in range(sources):
        column = jnp.sum(
            jnp.where(lane16 == row16, jnp.broadcast_to(charges[s], (16, 128)), 0.0), axis=1, keepdims=True
        )
        g = jnp.where(lane16 == 0, column, 0.0) * inside0
        b = divergence(g, east0, lower0) * inside0
        d = c0 * g
        impulse.append((g, b, c0 * g))

    def after(g, carry):
        for step in range(GROUP):
            k = g * GROUP + step
            q = wav_ref[k] * wav_ref[k]
            weight = quad_ref[k]
            diagonal = q * c + bottom + edge
            moments = {}
            for s in range(sources):
                ks = k * sources + s
                point, b, d = impulse[s]
                r = weight * point + nu[ks, :, 0:128]
                w = weight * (b + q * d) + nau[ks, :, 0:128]
                nu[ks, :, 0:128] = r
                nau[ks, :, 0:128] = w
                r8, w8 = r[:8], w[:8]
                whole = jnp.concatenate([w, nau[ks, :, half:]], axis=1)
                last_sum = energy(whole, east, lower, diagonal)[:, :128]
                for j, product in enumerate((r8 * r8, r8 * w8, w8 * w8, last_sum)):
                    moments[j, s] = product
            at = pl.ds(pl.multiple_of(k * 8, 8), 8)
            sums[0, at, :] = sums[0, at, :] + stack_sums([moments[j, s] for j in range(4) for s in range(sources)])
        return carry

    lax.fori_loop(0, chunks, after, 0)
    pay2[...] = row_sums(sums[0])[0:1, :]
    start_all(pay2, got2, send2, recv2)

    spread_weights(first, 0)
    spread_weights(second, 1)

    def totals(g, carry):
        for step in range(span):
            ks = g * span + step
            prim[ks] = prim[ks] + coef[0, pl.ds(ks, 1), :] * r0f[ks] + coef[1, pl.ds(ks, 1), :] * w0f[ks]
        return carry

    lax.fori_loop(0, chunks, totals, 0)
    sent_all(pay, got, send1, recv1)
    sent(sigma_halo())
    for g in range(chunks):
        sent(prim_halo(g))
        sent(prior_halo(g))

    wait_all(pay2, got2, send2, recv2)
    first, second = step_weights(jnp.sum(got2[:, 0, :], axis=0, keepdims=True), sources)
    spread_weights(first, 0)
    spread_weights(second, 1)
    last = lax.broadcasted_iota(jnp.int32, (8, depth), 1) == depth - 1

    def correlate(g, total):
        for step in range(GROUP):
            k = g * GROUP + step
            q = wav_ref[k] * wav_ref[k]
            for s in range(sources):
                ks = k * sources + s
                t = prim[ks]
                a = prior[ks] + coef[0, pl.ds(ks, 1), :] * nu[ks] + coef[1, pl.ds(ks, 1), :] * nau[ks]
                t_east, a_east = east_of(t)[:8], east_of(a)[:8]
                t, a = t[:8], a[:8]
                t_down = jnp.where(last, 0.0, pltpu.roll(t, depth - 1, 1))
                a_down = jnp.where(last, 0.0, pltpu.roll(a, depth - 1, 1))
                total = total + ((a_east - a) * (t_east - t) + (a_down - a) * (t_down - t) + q * a * t)
        return total

    grad_ref[...] = lax.fori_loop(0, chunks, correlate, jnp.zeros((8, depth), F32))
    sent_all(pay2, got2, send2, recv2)


def hand_over(pred_in, grad_in, pred_out, grad_out, sem):
    copies = [
        pltpu.make_async_copy(pred_in, pred_out, sem.at[0]),
        pltpu.make_async_copy(grad_in, grad_out, sem.at[1]),
    ]
    for copy in copies:
        copy.start()
    for copy in copies:
        copy.wait()


def on_device(n, primary, conductivity, wavenumbers, quadrature, electrodes, far_pole, observed, prior_adjoint):
    waves, sources, cols, depth = primary.shape
    fields = waves * sources
    per = electrodes.shape[0]
    vmem = pl.BlockSpec(memory_space=pltpu.VMEM)
    anywhere = pl.BlockSpec(memory_space=pl.ANY)
    wide = pltpu.VMEM((fields, 16, depth), F32)

    def edges(count):
        return pltpu.VMEM((fields, count, depth), F32)

    def sigma_edges(count):
        return pltpu.VMEM((count, depth), F32)

    dma = pltpu.SemaphoreType.DMA
    halos = 2 * (waves // GROUP) + 1
    results = pl.pallas_call(
        functools.partial(kernel, n),
        out_shape=(
            jax.ShapeDtypeStruct(observed.shape, F32),
            jax.ShapeDtypeStruct(conductivity.shape, F32),
        ),
        in_specs=[anywhere] * 8,
        out_specs=(vmem, vmem),
        scratch_shapes=[
            wide, wide, pltpu.VMEM((16, depth), F32),
            pltpu.SMEM((waves,), F32), pltpu.SMEM((waves,), F32), pltpu.SMEM((per,), jnp.int32),
            pltpu.VMEM(far_pole.shape, jnp.int32), pltpu.VMEM(observed.shape, F32),
            wide, wide, wide, wide,
            pltpu.VMEM((1 + per, 128, 128), F32),
            pltpu.VMEM((1 + per, 128), F32), pltpu.VMEM((n, 1 + per, 128), F32),
            pltpu.VMEM((1, 128), F32), pltpu.VMEM((n, 1, 128), F32),
            pltpu.VMEM((2, fields, depth), F32),
            dma((8,)), dma((halos,)), dma((halos,)), dma((halos,)), dma((halos,)), dma((n,)), dma((n,)), dma((n,)), dma((n,)),
            edges(LEFT), edges(RIGHT), edges(LEFT), edges(RIGHT), sigma_edges(LEFT), sigma_edges(RIGHT),
            edges(LEFT), edges(RIGHT), edges(LEFT), edges(RIGHT), sigma_edges(LEFT), sigma_edges(RIGHT),
        ],
        compiler_params=pltpu.CompilerParams(
            collective_id=0, has_side_effects=True, vmem_limit_bytes=56 * 1024 * 1024
        ),
    )(
        primary.reshape(fields, cols, depth), conductivity, wavenumbers, quadrature, electrodes, far_pole, observed,
        prior_adjoint.reshape(fields, cols, depth),
    )
    return pl.pallas_call(
        hand_over,
        out_shape=tuple(jax.ShapeDtypeStruct(r.shape, F32) for r in results),
        in_specs=[anywhere] * 2,
        out_specs=(anywhere, anywhere),
        scratch_shapes=[dma((2,))],
    )(*results)


def solution(mesh):
    placed = (
        P(None, "lines", "col", None), P("col", "lines"), P(), P(), P(("lines", "col")),
        P("lines", None), P("lines", None), P(None, "lines", "col", None),
    )
    return jax.shard_map(
        functools.partial(on_device, mesh.shape["col"]),
        mesh=mesh, in_specs=placed, out_specs=(P("lines", None), P("col", "lines")), check_vma=False,
    )
```
